256 devices in a mesh: pole: 4 (over y), node: 64 (over z, x, core).
Axes of the slice: x: 4, y: 4, z: 8, core: 2. Of those that a mesh axis runs over, the one named last changes fastest.
Arguments:
- dens_part: bfloat16 [4, 262144, 338], P('pole', 'node'), may hold values from -1.5 to 1.5
- dest_node: int32 [262144], P('node'), may hold values from 0 to 63, as said below
- pair_slot: int32 [262144], P('node'), may hold values from 0 to 1023, as said below
- deriv: bfloat16 [262144, 1014], P(('pole', 'node')), may hold values from -0.119628906 to 0.119628906
- pair_atoms: int32 [2, 262144], P(None, ('pole', 'node')), may hold values from 0 to 32767
Outputs:
- forces: float32 [3, 32768], P(None, ('pole', 'node'))
The draws below stay inside these ranges and needn't reach their ends.
Inputs may be any that keep to these rules, and one draw needn't show every extreme that they name: The share of block s is (s // 1024) % 4. Of the 1024 blocks of one share at most 32 have the same dest_node, and in every share exactly 32 do for some node index. Within one pole index, the number of blocks that a share on node n sends to node (n + k) % 64 depends on k alone. Every pair of pole index p and node index m receives exactly 1024 blocks of share p. `pair_slot`: the blocks of share p with dest_node m take each position of 0 to 1023 exactly once.
All inputs are finite; a program needn't handle non-finite values.
Results may differ from the reference program's by a relative error of at most 0.009.
Values may be sent and summed in bfloat16 or wider, within the bound.
No kernel may reach another device: no remote copies, remote signals or barrier semaphores. Data moves between devices by JAX's collectives and lax.ppermute only.
A program may use at most 64 MiB of HBM per device.

```python
import jax
import jax.numpy as jnp
from jax import lax

BSQ = 169
BLK_DEV = 1024
NB = 262144
ATOMS = 32768
CAP = 32
N_POLE = 4
N_NODE = 64


def routing(key):
    base_key = jax.random.fold_in(key, 7)
    k_off, k_cnt, k_send, k_recv = jax.random.split(base_key, 4)
    half_cap = CAP // 2
    offsets = jax.vmap(lambda subkey: jax.random.permutation(subkey, N_NODE)[:N_NODE - 1])(jax.random.split(k_off, N_POLE))
    pair_count = (N_NODE - 2) // 2
    spread = jax.random.randint(k_cnt, (N_POLE, pair_count), -(half_cap - 1), half_cap)
    counts = jnp.concatenate([jnp.full((N_POLE, 1), CAP, jnp.int32), half_cap + spread, half_cap - spread], axis=1).astype(jnp.int32)
    starts = jnp.cumsum(counts, axis=1) - counts
    position = jnp.arange(BLK_DEV, dtype=jnp.int32)
    run_index = jnp.sum((position[None, :, None] >= starts[:, None, 1:]).astype(jnp.int32), axis=2)
    offset_of = jnp.take_along_axis(offsets.astype(jnp.int32), run_index, axis=1)
    send_order = jax.vmap(lambda subkey: jax.random.permutation(subkey, BLK_DEV))(jax.random.split(k_send, N_POLE * N_NODE)).reshape(N_POLE, N_NODE, BLK_DEV).astype(jnp.int32)
    recv_order = jax.vmap(lambda subkey: jax.random.permutation(subkey, BLK_DEV))(jax.random.split(k_recv, N_POLE * N_NODE)).reshape(N_POLE, N_NODE, BLK_DEV).astype(jnp.int32)
    node_index = jnp.arange(N_NODE, dtype=jnp.int32)[None, :, None]
    pole_index = jnp.arange(N_POLE, dtype=jnp.int32)[:, None, None]
    offset_block = offset_of[pole_index, send_order]
    target_node = (node_index + offset_block) % N_NODE
    target_slot = recv_order[pole_index, target_node, send_order]
    target_node = jnp.transpose(target_node, (1, 0, 2)).reshape(-1).astype(jnp.int32)
    target_slot = jnp.transpose(target_slot, (1, 0, 2)).reshape(-1).astype(jnp.int32)
    return (target_node, target_slot)


def draw_dest_node(key, part):
    return routing(key)[0]


def draw_pair_slot(key, part):
    return routing(key)[1]


def touch_ends(drawn, stream_key, smallest, top_value):
    dims = drawn.shape
    place = [jax.random.randint(jax.random.fold_in(stream_key, axis), (), 0, dims[axis]) for axis in range(len(dims))]
    drawn = drawn.at[tuple(place)].set(smallest)
    longest = dims.index(max(dims))
    place[longest] = (place[longest] + 1) % dims[longest]
    return drawn.at[tuple(place)].set(top_value)


def block_scale(own_key, shape, shards, low, top_value):
    def one(dim, blocks):
        heights = jax.random.uniform(jax.random.fold_in(jax.random.fold_in(own_key, 6), dim), (blocks,), jnp.float32, low / len(shards), top_value / len(shards))
        return jnp.repeat(jnp.exp(heights), shape[dim] // blocks).reshape((-1,) + (1,) * (len(shape) - dim - 1))

    factor_of = one(*shards[0])
    for cut in shards[1:]:
        factor_of = factor_of * one(*cut)
    return factor_of


def noise(key, dims, width, reach, cuts=(), kind=jnp.bfloat16):
    drawn = jax.random.normal(key, dims, jnp.float32) * width
    if len(cuts) > 0:
        drawn = block_scale(key, dims, cuts, -0.22, 0.18) * drawn
    return jnp.clip(drawn, min=-reach, max=reach).astype(kind)


def setup_inputs(seed: int = 0) -> dict:
    streams_of = jax.random.split(jax.random.key(seed), 6)
    dens_part = noise(streams_of[0], (N_POLE, NB, 2 * BSQ), 0.25, 1.5, ((0, 4), (1, 64)))
    dest_node = draw_dest_node(jax.random.fold_in(streams_of[5], 71), 0)
    pair_slot = draw_pair_slot(jax.random.fold_in(streams_of[5], 71), 0)
    deriv = noise(streams_of[3], (NB, 6 * BSQ), 0.02, 0.119628906, ((0, 256),))
    pair_atoms = touch_ends(jax.random.randint(streams_of[4], (2, NB), 0, ATOMS), jax.random.fold_in(streams_of[4], 1), 0, ATOMS - 1).astype(jnp.int32)
    return dict(dens_part=dens_part, dest_node=dest_node, pair_slot=pair_slot, deriv=deriv, pair_atoms=pair_atoms)


def contract_tile(tiles):
    density_tile, deriv_tile = tiles
    density_tile = density_tile.astype(jnp.float32)
    deriv_tile = deriv_tile.astype(jnp.float32)
    grad_h = deriv_tile[:, : 3 * BSQ].reshape(-1, 3, BSQ)
    grad_s = deriv_tile[:, 3 * BSQ:].reshape(-1, 3, BSQ)
    first = jnp.einsum("bk,bck->bc", density_tile[:, :BSQ], grad_h, precision=lax.Precision.HIGHEST)
    second = jnp.einsum("bk,bck->bc", density_tile[:, BSQ:], grad_s, precision=lax.Precision.HIGHEST)
    return first - second


def reference(dens_part, dest_node, pair_slot, deriv, pair_atoms):
    summed = jnp.sum(dens_part.astype(jnp.float32), axis=0).astype(jnp.bfloat16)
    block_index = jnp.arange(NB, dtype=jnp.int32)
    share_index = (block_index // BLK_DEV) % N_POLE
    target = ((share_index * N_NODE + dest_node) * BLK_DEV + pair_slot).astype(jnp.int32)
    pair_dens = jnp.zeros_like(summed).at[target].set(summed)
    groups = NB // BLK_DEV
    pair_term = lax.map(contract_tile, (pair_dens.reshape(groups, BLK_DEV, 2 * BSQ), deriv.reshape(groups, BLK_DEV, 6 * BSQ)))
    pair_term = pair_term.reshape(NB, 3)
    forces_out = jnp.zeros((3, ATOMS), jnp.float32)
    forces_out = forces_out.at[:, pair_atoms[0]].add(-2.0 * pair_term.T)
    forces_out = forces_out.at[:, pair_atoms[1]].add(2.0 * pair_term.T)
    return forces_out
```

```python
import functools

import jax
import jax.numpy as jnp
from jax import lax
from jax.experimental import pallas as pl
from jax.experimental.pallas import tpu as pltpu
from jax.sharding import PartitionSpec as P

ATOM_DEV = 128
LANES = 128
BASE = 32
F32 = jnp.float32
BF16 = jnp.bfloat16


def iota(shape, dim):
    return lax.broadcasted_iota(jnp.int32, shape, dim)


def params(mib=48):
    return pltpu.CompilerParams(vmem_limit_bytes=mib * 1024 * 1024)


def cost(flops, nbytes):
    return pl.CostEstimate(flops=flops, bytes_accessed=nbytes, transcendentals=0)


def plan_kernel(capacity, node_row, node_col, place):
    blocks = node_row.shape[1]
    tile = min(256, blocks)
    row = node_row[...]
    rank = jnp.zeros((1, blocks), F32)
    for start in range(0, blocks, tile):
        col = node_col[start : start + tile, :]
        earlier = iota((tile, blocks), 0) + start < iota((tile, blocks), 1)
        same = jnp.where((col == row) & earlier, 1.0, 0.0)
        rank = rank + jnp.sum(same, axis=0, keepdims=True)
    place[...] = row * capacity + rank.astype(jnp.int32)


def deriv_kernel(half, deriv, out):
    rows = deriv.shape[0]
    wide = out.shape[2]
    values = deriv[...].astype(F32)
    for c in range(3):
        first = values[:, c * half : (c + 1) * half]
        second = -values[:, (3 + c) * half : (4 + c) * half]
        rest = jnp.zeros((rows, wide - 2 * half), F32)
        out[c] = jnp.concatenate([first, second, rest], axis=1).astype(BF16)


def pack_kernel(width, place, slot_col, own, low, high, out, dens):
    blocks = own.shape[0]
    wide = out.shape[1]
    half = blocks // 2
    extra = jnp.zeros((half, wide - width), F32)
    for part, arrived in ((0, low), (1, high)):
        rows = pl.ds(part * half, half)
        total = own[rows, :].astype(F32) + arrived[...].astype(F32)
        total = jnp.concatenate([total, extra], axis=1)
        slot = slot_col[rows, :]
        lane = iota((half, wide), 1)
        total = jnp.where(lane == width, (slot // BASE + 1).astype(F32), total)
        total = jnp.where(lane == width + 1, (slot % BASE).astype(F32), total)
        dens[rows, :] = total.astype(BF16)
    tile = min(256, out.shape[0])
    where = place[...]
    for start in range(0, out.shape[0], tile):
        pick = jnp.where(iota((tile, blocks), 0) + start == where, 1.0, 0.0)
        moved = jnp.dot(pick.astype(BF16), dens[...], preferred_element_type=F32)
        out[start : start + tile, :] = moved.astype(BF16)


def force_kernel(width, arrived, deriv, atoms_row, atoms_col, out, total):
    blocks = deriv.shape[1]
    slots, wide = arrived.shape
    owners = out.shape[0]
    pick_cols = (iota((8, wide), 1) == iota((8, wide), 0) + width) & (iota((8, wide), 0) < 2)
    picker = jnp.where(pick_cols, 1.0, 0.0).astype(BF16)
    coded = lax.dot_general(
        picker, arrived[...], (((1,), (1,)), ((), ())), preferred_element_type=F32
    )
    slot_row = ((coded[0:1, :] - 1.0) * BASE + coded[1:2, :]).astype(jnp.int32)
    tile = min(256, blocks)
    for start in range(0, blocks, tile):
        pick = jnp.where(iota((tile, slots), 0) + start == slot_row, 1.0, 0.0)
        dens = jnp.dot(pick.astype(BF16), arrived[...], preferred_element_type=F32)
        hi = atoms_row[:, start : start + tile] // ATOM_DEV
        lo = atoms_col[start : start + tile, :] % ATOM_DEV
        place_lo = [iota((tile, ATOM_DEV), 1) == lo[:, e : e + 1] for e in range(2)]
        weighted = [[], []]
        for c in range(3):
            prod = dens * deriv[c, start : start + tile, :].astype(F32)
            term = jnp.sum(prod, axis=1, keepdims=True)
            for e, sign in ((0, -2.0), (1, 2.0)):
                weighted[e].append(jnp.where(place_lo[e], sign * term, 0.0).astype(BF16))
        added = jnp.zeros((owners, 3 * ATOM_DEV), F32)
        for e in range(2):
            rows = jnp.where(iota((owners, tile), 0) == hi[e : e + 1, :], 1.0, 0.0)
            added = added + jnp.dot(
                rows.astype(BF16), jnp.concatenate(weighted[e], axis=1), preferred_element_type=F32
            )
        if start == 0:
            total[...] = added
        else:
            total[...] += added
    out[...] = total[...].astype(BF16)


def body(dens_part, dest_node, pair_slot, deriv, pair_atoms):
    blocks = deriv.shape[0]
    width = dens_part.shape[2]
    half_width = width // 2
    wide = (width + 2 + LANES - 1) // LANES * LANES
    nodes = lax.axis_size("node")
    poles = lax.axis_size("pole")
    pole = lax.axis_index("pole")
    capacity = 2 * blocks // nodes
    slots = nodes * capacity
    owners = poles * nodes
    half = blocks // 2
    partials = dens_part[0]

    def part(share, which):
        first = lax.rem(share, poles) * blocks + which * half
        return lax.dynamic_slice(partials, (first, 0), (half, width))

    up = [(k, (k + 1) % poles) for k in range(poles)]
    down = [(k, (k - 1) % poles) for k in range(poles)]
    with jax.named_scope("pole_sum"):
        low = lax.ppermute(part(pole + poles - 1, 0), "pole", up)
        high = lax.ppermute(part(pole + 1, 1), "pole", down)
        for step in range(2, poles):
            low = (low.astype(F32) + part(pole + poles - step, 0).astype(F32)).astype(BF16)
            high = (high.astype(F32) + part(pole + step, 1).astype(F32)).astype(BF16)
            low = lax.ppermute(low, "pole", up)
            high = lax.ppermute(high, "pole", down)
        own = lax.dynamic_slice(partials, (pole * blocks, 0), (blocks, width))

    target_node = lax.dynamic_slice_in_dim(dest_node, pole * blocks, blocks, 0)
    target_slot = lax.dynamic_slice_in_dim(pair_slot, pole * blocks, blocks, 0)
    place = pl.pallas_call(
        functools.partial(plan_kernel, capacity),
        out_shape=jax.ShapeDtypeStruct((1, blocks), jnp.int32),
        compiler_params=params(),
        cost_estimate=cost(6 * blocks * blocks, 8 * blocks),
        name="placement",
    )(target_node.reshape(1, blocks), target_node.reshape(blocks, 1))

    tile = min(256, blocks)
    aligned = pl.pallas_call(
        functools.partial(deriv_kernel, half_width),
        grid=(blocks // tile,),
        in_specs=[pl.BlockSpec((tile, deriv.shape[1]), lambda i: (i, 0))],
        out_specs=pl.BlockSpec((3, tile, wide), lambda i: (0, i, 0)),
        out_shape=jax.ShapeDtypeStruct((3, blocks, wide), BF16),
        compiler_params=params(),
        cost_estimate=cost(6 * blocks * wide, 4 * blocks * deriv.shape[1]),
        name="align_derivatives",
    )(deriv)

    outgoing = pl.pallas_call(
        functools.partial(pack_kernel, width),
        out_shape=jax.ShapeDtypeStruct((slots, wide), BF16),
        scratch_shapes=[pltpu.VMEM((blocks, wide), BF16)],
        compiler_params=params(),
        cost_estimate=cost(2 * slots * blocks * wide, 2 * (slots + 2 * blocks) * wide),
        name="pack_density",
    )(place, target_slot.reshape(blocks, 1), own, low, high)

    with jax.named_scope("route_density"):
        arrived = lax.all_to_all(
            outgoing.reshape(nodes, capacity, wide), "node", 0, 0, tiled=True
        ).reshape(slots, wide)

    partial_forces = pl.pallas_call(
        functools.partial(force_kernel, width),
        out_shape=jax.ShapeDtypeStruct((owners, 3 * ATOM_DEV), BF16),
        scratch_shapes=[pltpu.VMEM((owners, 3 * ATOM_DEV), F32)],
        compiler_params=params(),
        cost_estimate=cost(2 * slots * blocks * wide, 2 * (slots + 3 * blocks) * wide),
        name="contract_and_scatter",
    )(arrived, aligned, pair_atoms, pair_atoms.T)

    with jax.named_scope("force_exchange"):
        gathered = lax.all_to_all(
            partial_forces.reshape(owners, 3, ATOM_DEV), ("pole", "node"), 0, 0, tiled=True
        )
        return jnp.sum(gathered.astype(F32), axis=0)


def solution(mesh):
    return jax.shard_map(
        body,
        mesh=mesh,
        in_specs=(
            P("pole", "node", None),
            P("node"),
            P("node"),
            P(("pole", "node"), None),
            P(None, ("pole", "node")),
        ),
        out_specs=P(None, ("pole", "node")),
        check_vma=False,
    )
```

```python
import functools

import jax
import jax.numpy as jnp
from jax import lax
from jax.experimental import pallas as pl
from jax.experimental.pallas import tpu as pltpu
from jax.sharding import PartitionSpec as P

ATOM_DEV = 128
LANES = 128
BASE = 32
F32 = jnp.float32
BF16 = jnp.bfloat16


def iota(shape, dim):
    return lax.broadcasted_iota(jnp.int32, shape, dim)


def params(mib=16):
    return pltpu.CompilerParams(vmem_limit_bytes=mib * 1024 * 1024)


def cost(flops, nbytes):
    return pl.CostEstimate(flops=flops, bytes_accessed=nbytes, transcendentals=0)


def one_hot(row, start, rows):
    found = iota((rows, row.shape[1]), 0) + start == row
    return jnp.where(found, 1.0, 0.0).astype(BF16)


def rows_times(a, b):
    return lax.dot_general(a, b, (((1,), (1,)), ((), ())), preferred_element_type=F32)


def plan_kernel(capacity, node_row, node_col, pick, where):
    slots, blocks = pick.shape
    tile = min(256, blocks)
    row = node_row[...]
    rank = jnp.zeros((1, blocks), F32)
    for start in range(0, blocks, tile):
        col = node_col[start : start + tile, :]
        earlier = iota((tile, blocks), 0) + start < iota((tile, blocks), 1)
        same = jnp.where((col == row) & earlier, 1.0, 0.0)
        rank = rank + jnp.sum(same, axis=0, keepdims=True)
    place = row * capacity + rank.astype(jnp.int32)
    where[...] = place
    for start in range(0, slots, tile):
        pick[start : start + tile, :] = one_hot(place, start, tile)


def deriv_kernel(half, deriv, out_second, out_first):
    rows = deriv.shape[0]
    split = out_second.shape[2]
    wide = split + out_first.shape[2]
    values = deriv[...].astype(F32)
    for c in range(3):
        first = values[:, c * half : (c + 1) * half]
        second = -values[:, (3 + c) * half : (4 + c) * half]
        rest = jnp.zeros((rows, wide - 2 * half), F32)
        line = jnp.concatenate([first, second, rest], axis=1).astype(BF16)
        out_second[c] = line[:, :split]
        out_first[c] = line[:, split:]


def pole_total(parts):
    total = parts[0][...].astype(F32)
    for other in parts[1:]:
        total = total + other[...].astype(F32)
    return total


def pack_first_kernel(pick, slot_row, *refs):
    *parts, out, dens = refs
    columns = parts[0].shape[0]
    wide = dens.shape[0]
    slot = slot_row[...]
    dens[columns:, :] = jnp.zeros((wide - columns, dens.shape[1]), F32)
    dens[:columns, :] = pole_total(parts)
    dens[columns : columns + 1, :] = (slot // BASE + 1).astype(F32)
    dens[columns + 1 : columns + 2, :] = (slot % BASE).astype(F32)
    total = dens[...].astype(BF16)
    tile = min(256, out.shape[0])
    for start in range(0, out.shape[0], tile):
        rows = pick[start : start + tile, :]
        out[start : start + tile, :] = rows_times(rows, total).astype(BF16)


def pack_second_kernel(where, *refs):
    *parts, out = refs
    total = pole_total(parts).astype(BF16)
    place = where[...]
    tile = min(256, out.shape[0])
    for start in range(0, out.shape[0], tile):
        rows = one_hot(place, start, tile)
        out[start : start + tile, :] = rows_times(rows, total).astype(BF16)


def row_terms(dens, deriv, start):
    rows, wide = dens.shape
    ones = jnp.ones((8, LANES), BF16)
    terms = []
    for c in range(3):
        prod = dens * deriv[c, start : start + rows, :].astype(F32)
        folded = prod[:, :LANES]
        for first in range(LANES, wide, LANES):
            folded = folded + prod[:, first : first + LANES]
        large = folded.astype(BF16)
        small = (folded - large.astype(F32)).astype(BF16)
        terms.append((rows_times(ones, large) + rows_times(ones, small))[0:1, :])
    return terms


def contract_first_kernel(columns, arrived, deriv, atoms, info):
    blocks = atoms.shape[1]
    slots, wide = arrived.shape
    line = iota((8, wide), 0)
    picker = jnp.where((iota((8, wide), 1) == line + columns) & (line < 2), 1.0, 0.0)
    coded = rows_times(picker.astype(BF16), arrived[...])
    slot_row = (coded[0:1, :] - 1.0) * BASE + coded[1:2, :]
    info[...] = jnp.zeros_like(info)
    info[3:4, :] = slot_row
    info[4:6, :blocks] = atoms[...].astype(F32)
    slot_row = slot_row.astype(jnp.int32)
    tile = min(256, blocks)
    for start in range(0, blocks, tile):
        dens = jnp.dot(
            one_hot(slot_row, start, tile), arrived[...], preferred_element_type=F32
        )
        for c, term in enumerate(row_terms(dens, deriv, start)):
            info[c : c + 1, start : start + tile] = term


def force_kernel(arrived, deriv, info, out, total):
    blocks = deriv.shape[1]
    owners = out.shape[0]
    slot_row = info[3:4, :].astype(jnp.int32)
    tile = min(256, blocks)
    for start in range(0, blocks, tile):
        dens = jnp.dot(
            one_hot(slot_row, start, tile), arrived[...], preferred_element_type=F32
        )
        terms = row_terms(dens, deriv, start)
        added = None
        for e, sign in ((0, -2.0), (1, 2.0)):
            atom = info[4 + e : 5 + e, start : start + tile].astype(jnp.int32)
            found = iota((ATOM_DEV, tile), 0) == atom % ATOM_DEV
            weighted = []
            for c in range(3):
                term = sign * (terms[c] + info[c : c + 1, start : start + tile])
                weighted.append(jnp.where(found, term, 0.0).astype(BF16))
            owner = one_hot(atom // ATOM_DEV, 0, owners)
            moved = rows_times(owner, jnp.concatenate(weighted, axis=0))
            added = moved if added is None else added + moved
        if start == 0:
            total[...] = added
        else:
            total[...] += added
    out[...] = total[...].astype(BF16)


def body(dens_part, dest_node, pair_slot, deriv, pair_atoms):
    blocks = deriv.shape[0]
    width = dens_part.shape[2]
    half_width = width // 2
    split = width // LANES * LANES
    last = width - split
    wide = (last + 2 + LANES - 1) // LANES * LANES
    nodes = lax.axis_size("node")
    poles = lax.axis_size("pole")
    pole = lax.axis_index("pole")
    capacity = 2 * blocks // nodes
    slots = nodes * capacity
    owners = poles * nodes
    partials = dens_part[0].T

    def exchange(first_column, columns):
        def share(which):
            start = lax.rem(pole + which, poles) * blocks
            return lax.dynamic_slice(partials, (first_column, start), (columns, blocks))

        parts = []
        for step in (1, 3, 2):
            pairs = [(k, (k + step) % poles) for k in range(poles)]
            parts.append(lax.ppermute(share(step), "pole", pairs))
        return [share(0)] + parts

    with jax.named_scope("pole_exchange_first"):
        parts_first = exchange(split, last)
    with jax.named_scope("pole_exchange_second"):
        parts_second = exchange(0, split)

    target_node = lax.dynamic_slice_in_dim(dest_node, pole * blocks, blocks, 0)
    target_slot = lax.dynamic_slice_in_dim(pair_slot, pole * blocks, blocks, 0)
    pick_out, place = pl.pallas_call(
        functools.partial(plan_kernel, capacity),
        out_shape=[
            jax.ShapeDtypeStruct((slots, blocks), BF16),
            jax.ShapeDtypeStruct((1, blocks), jnp.int32),
        ],
        compiler_params=params(),
        cost_estimate=cost(6 * blocks * blocks, 2 * slots * blocks),
        name="placement",
    )(target_node.reshape(1, blocks), target_node.reshape(blocks, 1))

    tile = min(256, blocks)
    deriv_second, deriv_first = pl.pallas_call(
        functools.partial(deriv_kernel, half_width),
        grid=(blocks // tile,),
        in_specs=[pl.BlockSpec((tile, deriv.shape[1]), lambda i: (i, 0))],
        out_specs=[
            pl.BlockSpec((3, tile, split), lambda i: (0, i, 0)),
            pl.BlockSpec((3, tile, wide), lambda i: (0, i, 0)),
        ],
        out_shape=[
            jax.ShapeDtypeStruct((3, blocks, split), BF16),
            jax.ShapeDtypeStruct((3, blocks, wide), BF16),
        ],
        compiler_params=params(),
        cost_estimate=cost(6 * blocks * width, 4 * blocks * deriv.shape[1]),
        name="align_derivatives",
    )(deriv)

    def route(packed):
        columns = packed.shape[1]
        moved = lax.all_to_all(
            packed.reshape(nodes, capacity, columns), "node", 0, 0, tiled=True
        )
        return moved.reshape(slots, columns)

    packed_first = pl.pallas_call(
        pack_first_kernel,
        out_shape=jax.ShapeDtypeStruct((slots, wide), BF16),
        scratch_shapes=[pltpu.VMEM((wide, blocks), F32)],
        compiler_params=params(),
        cost_estimate=cost(16 * slots * blocks * wide, 16 * slots * blocks),
        name="pack_first",
    )(pick_out, target_slot.reshape(1, blocks), *parts_first)
    with jax.named_scope("route_first"):
        arrived_first = route(packed_first)

    packed_second = pl.pallas_call(
        pack_second_kernel,
        out_shape=jax.ShapeDtypeStruct((slots, split), BF16),
        compiler_params=params(),
        cost_estimate=cost(200 * slots * blocks * split, 200 * slots * blocks),
        name="pack_second",
    )(place, *parts_second)
    with jax.named_scope("route_second"):
        arrived_second = route(packed_second)

    info = pl.pallas_call(
        functools.partial(contract_first_kernel, last),
        out_shape=jax.ShapeDtypeStruct((8, slots), F32),
        compiler_params=params(),
        cost_estimate=cost(2 * slots * blocks * wide, 2 * slots * blocks),
        name="contract_first",
    )(arrived_first, deriv_first, pair_atoms)

    partial_forces = pl.pallas_call(
        force_kernel,
        out_shape=jax.ShapeDtypeStruct((owners, 3 * ATOM_DEV), BF16),
        scratch_shapes=[pltpu.VMEM((owners, 3 * ATOM_DEV), F32)],
        compiler_params=params(),
        cost_estimate=cost(2 * slots * blocks * split, 2 * slots * blocks),
        name="contract_and_scatter",
    )(arrived_second, deriv_second, info)

    with jax.named_scope("force_exchange"):
        gathered = lax.all_to_all(
            partial_forces.reshape(owners, 3, ATOM_DEV), ("pole", "node"), 0, 0, tiled=True
        )
        return jnp.sum(gathered.astype(F32), axis=0)


def solution(mesh):
    return jax.shard_map(
        body,
        mesh=mesh,
        in_specs=(
            P("pole", "node", None),
            P("node"),
            P("node"),
            P(("pole", "node"), None),
            P(None, ("pole", "node")),
        ),
        out_specs=P(None, ("pole", "node")),
        check_vma=False,
    )
```

```python
import functools

import jax
import jax.numpy as jnp
from jax import lax
from jax.experimental import pallas as pl
from jax.experimental.pallas import tpu as pltpu
from jax.sharding import PartitionSpec as P

ATOM_DEV = 128
LANES = 128
BASE = 32
F32 = jnp.float32
BF16 = jnp.bfloat16


def iota(shape, dim):
    return lax.broadcasted_iota(jnp.int32, shape, dim)


def params(mib=16):
    return pltpu.CompilerParams(vmem_limit_bytes=mib * 1024 * 1024)


def cost(flops, nbytes):
    return pl.CostEstimate(flops=flops, bytes_accessed=nbytes, transcendentals=0)


def one_hot(row, start, rows):
    line = lax.broadcasted_iota(jnp.int16, (rows, row.shape[1]), 0)
    found = line == (row - start).astype(jnp.int16)
    return jnp.where(found, jnp.ones((), BF16), jnp.zeros((), BF16))


def rows_times(a, b):
    return lax.dot_general(a, b, (((1,), (1,)), ((), ())), preferred_element_type=F32)


def plan_kernel(capacity, nodes, pole, node, slot, pick, where, slot_row):
    slots, blocks = pick.shape
    here = pole[0]
    slot_row[...] = slot[pl.ds(here, 1), :]
    row = node[pl.ds(here, 1), :]
    tile = min(256, blocks)
    earlier = jnp.where(iota((tile, tile), 0) < iota((tile, tile), 1), 1.0, 0.0).astype(BF16)
    seen = jnp.zeros((nodes, 1), F32)
    for start in range(0, blocks, tile):
        part = row[:, start : start + tile]
        same = jnp.where(iota((nodes, tile), 0) == part, 1.0, 0.0)
        before = jnp.dot(same.astype(BF16), earlier, preferred_element_type=F32) + seen
        rank = jnp.sum(same * before, axis=0, keepdims=True).astype(jnp.int32)
        where[:, start : start + tile] = part * capacity + rank
        seen = seen + jnp.sum(same, axis=1, keepdims=True)
    place = where[...]
    for start in range(0, slots, tile):
        pick[start : start + tile, :] = one_hot(place, start, tile)


def deriv_kernel(half, deriv, out_second, out_first):
    rows = deriv.shape[0]
    split = out_second.shape[2]
    wide = split + out_first.shape[2]
    values = deriv[...].astype(F32)
    for c in range(3):
        first = values[:, c * half : (c + 1) * half]
        second = -values[:, (3 + c) * half : (4 + c) * half]
        rest = jnp.zeros((rows, wide - 2 * half), F32)
        line = jnp.concatenate([first, second, rest], axis=1).astype(BF16)
        out_second[c] = line[:, :split]
        out_first[c] = line[:, split:]


def pole_total(parts):
    total = parts[0][...].astype(F32)
    for other in parts[1:]:
        total = total + other[...].astype(F32)
    return total


def pack_first_kernel(pick, slot_row, *refs):
    *parts, out, dens, rows, sem = refs
    columns = parts[0].shape[0]
    wide = dens.shape[0]
    slot = slot_row[...]
    dens[columns:, :] = jnp.zeros((wide - columns, dens.shape[1]), F32)
    dens[:columns, :] = pole_total(parts)
    dens[columns : columns + 1, :] = (slot // BASE + 1).astype(F32)
    dens[columns + 1 : columns + 2, :] = (slot % BASE).astype(F32)
    total = dens[...].astype(BF16)
    tile = min(512, rows.shape[0])
    copies = []
    for start in range(0, rows.shape[0], tile):
        part = pl.ds(start, tile)
        rows[part, :] = rows_times(pick[part, :], total).astype(BF16)
        copies.append(
            pltpu.make_async_copy(rows.at[part, :], out.at[part, :], sem.at[start // tile])
        )
        copies[-1].start()
    for copy in copies:
        copy.wait()


def pack_second_kernel(capacity, core, where, *refs):
    *parts, same, other = refs
    total = pole_total(parts).astype(BF16)
    place = where[...]
    block, rank = place // capacity, place % capacity
    row = block // 2 * capacity + rank
    tile = min(512, same.shape[0])
    for out, whose in ((other, 1 - core[0]), (same, core[0])):
        wanted = jnp.where(block % 2 == whose, row, -1)
        for start in range(0, out.shape[0], tile):
            rows = one_hot(wanted, start, tile)
            out[start : start + tile, :] = rows_times(rows, total).astype(BF16)


def row_terms(dens, deriv, start):
    rows, wide = dens.shape
    ones = jnp.ones((8, LANES), BF16)
    terms = []
    for c in range(3):
        prod = dens * deriv[c, start : start + rows, :].astype(F32)
        folded = prod[:, :LANES]
        for first in range(LANES, wide, LANES):
            folded = folded + prod[:, first : first + LANES]
        large = folded.astype(BF16)
        small = (folded - large.astype(F32)).astype(BF16)
        terms.append((rows_times(ones, large) + rows_times(ones, small))[0:1, :])
    return terms


def contract_first_kernel(columns, capacity, core, arrived, deriv, atoms, info):
    blocks = atoms.shape[1]
    slots, wide = arrived.shape
    line = iota((8, wide), 0)
    picker = jnp.where((iota((8, wide), 1) == line + columns) & (line < 2), 1.0, 0.0)
    coded = rows_times(picker.astype(BF16), arrived[...])
    slot_row = (coded[0:1, :] - 1.0) * BASE + coded[1:2, :]
    info[...] = jnp.zeros_like(info)
    line = jnp.broadcast_to(slot_row, info.shape)
    ahead = pltpu.roll(line, slots - capacity, 1)
    behind = pltpu.roll(line, capacity, 1)
    swapped = jnp.where(iota(info.shape, 1) % (2 * capacity) < capacity, ahead, behind)
    info[3:4, :] = jnp.where(core[0] == 0, line, swapped)[0:1, :]
    info[4:6, :blocks] = atoms[...].astype(F32)
    slot_row = slot_row.astype(jnp.int32)
    tile = min(256, blocks)
    for start in range(0, blocks, tile):
        dens = jnp.dot(
            one_hot(slot_row, start, tile), arrived[...], preferred_element_type=F32
        )
        for c, term in enumerate(row_terms(dens, deriv, start)):
            info[c : c + 1, start : start + tile] = term


def force_kernel(arrived, source, info, out, total, deriv, sem):
    blocks = deriv.shape[1]
    owners = out.shape[1]
    slot_row = info[3:4, :].astype(jnp.int32)
    tile = min(512, blocks)
    copies = []
    for i in range(blocks // tile):
        rows = pl.ds(i * tile, tile)
        copies.append(
            pltpu.make_async_copy(source.at[:, rows, :], deriv.at[:, rows, :], sem.at[i])
        )
        copies[i].start()
    for start in range(0, blocks, tile):
        dens = jnp.dot(
            one_hot(slot_row, start, tile), arrived[...], preferred_element_type=F32
        )
        copies[start // tile].wait()
        terms = row_terms(dens, deriv, start)
        added = None
        for e, sign in ((0, -2.0), (1, 2.0)):
            atom = info[4 + e : 5 + e, start : start + tile].astype(jnp.int32)
            found = iota((ATOM_DEV, tile), 0) == atom % ATOM_DEV
            weighted = []
            for c in range(3):
                term = sign * (terms[c] + info[c : c + 1, start : start + tile])
                weighted.append(jnp.where(found, term, 0.0).astype(BF16))
            owner = one_hot(atom // ATOM_DEV, 0, owners)
            moved = rows_times(owner, jnp.concatenate(weighted, axis=0))
            added = moved if added is None else added + moved
        if start == 0:
            total[...] = added
        else:
            total[...] += added
    for c in range(3):
        out[c] = total[:, c * ATOM_DEV : (c + 1) * ATOM_DEV].astype(BF16)


def body(dens_part, dest_node, pair_slot, deriv, pair_atoms):
    blocks = deriv.shape[0]
    width = dens_part.shape[2]
    half_width = width // 2
    split = width // LANES * LANES
    last = width - split
    wide = (last + 2 + LANES - 1) // LANES * LANES
    nodes = lax.axis_size("node")
    poles = lax.axis_size("pole")
    pole = lax.axis_index("pole")
    capacity = 2 * blocks // nodes
    slots = nodes * capacity
    owners = poles * nodes
    partials = dens_part[0].T

    def exchange(first_column, columns):
        def share(which):
            start = lax.rem(pole + which, poles) * blocks
            return lax.dynamic_slice(partials, (first_column, start), (columns, blocks))

        parts = []
        for step in (1, 3, 2):
            pairs = [(k, (k + step) % poles) for k in range(poles)]
            parts.append(lax.ppermute(share(step), "pole", pairs))
        return parts

    with jax.named_scope("pole_exchange_first"):
        parts_first = exchange(split, last)
        parts_first.append(
            lax.dynamic_slice(partials, (split, pole * blocks), (last, blocks))
        )
    with jax.named_scope("pole_exchange_second"):
        parts_second = exchange(0, split)

    whole = pl.BlockSpec(memory_space=pltpu.VMEM)
    scalar = pl.BlockSpec(memory_space=pltpu.SMEM)
    pick_out, place, slot_row = pl.pallas_call(
        functools.partial(plan_kernel, capacity, nodes),
        in_specs=[scalar, whole, whole],
        out_shape=[
            jax.ShapeDtypeStruct((slots, blocks), BF16),
            jax.ShapeDtypeStruct((1, blocks), jnp.int32),
            jax.ShapeDtypeStruct((1, blocks), jnp.int32),
        ],
        compiler_params=params(),
        cost_estimate=cost(6 * blocks * blocks, 2 * slots * blocks),
        name="placement",
    )(pole.reshape(1), dest_node.reshape(poles, blocks), pair_slot.reshape(poles, blocks))

    tile = min(256, blocks)
    deriv_second, deriv_first = pl.pallas_call(
        functools.partial(deriv_kernel, half_width),
        grid=(blocks // tile,),
        in_specs=[pl.BlockSpec((tile, deriv.shape[1]), lambda i: (i, 0))],
        out_specs=[
            pl.BlockSpec((3, tile, split), lambda i: (0, i, 0)),
            pl.BlockSpec((3, tile, wide), lambda i: (0, i, 0)),
        ],
        out_shape=[
            pltpu.HBM((3, blocks, split), BF16),
            jax.ShapeDtypeStruct((3, blocks, wide), BF16),
        ],
        compiler_params=params(),
        cost_estimate=cost(6 * blocks * width, 4 * blocks * deriv.shape[1]),
        name="align_derivatives",
    )(deriv)

    def route(packed):
        columns = packed.shape[1]
        moved = lax.all_to_all(
            packed.reshape(nodes, capacity, columns), "node", 0, 0, tiled=True
        )
        return moved.reshape(slots, columns)

    packed_first = pl.pallas_call(
        pack_first_kernel,
        out_shape=jax.ShapeDtypeStruct((slots, wide), BF16),
        out_specs=pl.BlockSpec(memory_space=pltpu.HBM),
        scratch_shapes=[
            pltpu.VMEM((wide, blocks), F32),
            pltpu.VMEM((slots, wide), BF16),
            pltpu.SemaphoreType.DMA((max(1, slots // 512),)),
        ],
        compiler_params=params(),
        cost_estimate=cost(16 * slots * blocks * wide, 16 * slots * blocks),
        name="pack_first",
    )(pick_out, slot_row, *parts_first)
    with jax.named_scope("pole_exchange_second"):
        later, packed_first = lax.optimization_barrier((partials, packed_first))
        parts_second.append(
            lax.dynamic_slice(later, (0, pole * blocks), (split, blocks))
        )
    with jax.named_scope("route_first"):
        arrived_first = route(packed_first)

    core = lax.rem(lax.axis_index("node"), 2)
    half = jax.ShapeDtypeStruct((slots // 2, split), BF16)
    same_core, other_core = pl.pallas_call(
        functools.partial(pack_second_kernel, capacity),
        in_specs=[scalar] + [whole] * (1 + len(parts_second)),
        out_shape=[half, half],
        compiler_params=params(),
        cost_estimate=cost(200 * slots * blocks * split, 200 * slots * blocks),
        name="pack_second",
    )(core.reshape(1), place, *parts_second)
    with jax.named_scope("route_second"):
        sibling = lax.ppermute(other_core, "node", [(k, k ^ 1) for k in range(nodes)])
        chips = nodes // 2
        both = jnp.concatenate(
            [x.reshape(chips, capacity, split) for x in (same_core, sibling)], axis=1
        )
        groups = [list(range(c, nodes, 2)) for c in range(2)]
        arrived_second = lax.all_to_all(
            both, "node", 0, 0, axis_index_groups=groups, tiled=True
        ).reshape(slots, split)

    info = pl.pallas_call(
        functools.partial(contract_first_kernel, last, capacity),
        in_specs=[scalar, whole, whole, whole],
        out_shape=jax.ShapeDtypeStruct((8, slots), F32),
        compiler_params=params(),
        cost_estimate=cost(2 * slots * blocks * wide, 2 * slots * blocks),
        name="contract_first",
    )(core.reshape(1), arrived_first, deriv_first, pair_atoms)

    partial_forces = pl.pallas_call(
        force_kernel,
        in_specs=[whole, pl.BlockSpec(memory_space=pltpu.HBM), whole],
        out_shape=jax.ShapeDtypeStruct((3, owners, ATOM_DEV), BF16),
        scratch_shapes=[
            pltpu.VMEM((owners, 3 * ATOM_DEV), F32),
            pltpu.VMEM((3, blocks, split), BF16),
            pltpu.SemaphoreType.DMA((max(1, blocks // 512),)),
        ],
        compiler_params=params(),
        cost_estimate=cost(2 * slots * blocks * split, 2 * slots * blocks),
        name="contract_and_scatter",
    )(arrived_second, pltpu.with_memory_space_constraint(deriv_second, pltpu.HBM), info)

    with jax.named_scope("force_exchange"):
        gathered = lax.all_to_all(
            jnp.transpose(partial_forces, (1, 0, 2)), ("pole", "node"), 0, 0, tiled=True
        )
        return jnp.sum(gathered.astype(F32), axis=0)


def solution(mesh):
    return jax.shard_map(
        body,
        mesh=mesh,
        in_specs=(
            P("pole", "node", None),
            P("node"),
            P("node"),
            P(("pole", "node"), None),
            P(None, ("pole", "node")),
        ),
        out_specs=P(None, ("pole", "node")),
        check_vma=False,
    )
```

```python
import functools

import jax
import jax.numpy as jnp
from jax import lax
from jax.experimental import pallas as pl
from jax.experimental.pallas import tpu as pltpu
from jax.sharding import PartitionSpec as P

ATOM_DEV = 128
LANES = 128
BASE = 32
F32 = jnp.float32
BF16 = jnp.bfloat16


def iota(shape, dim):
    return lax.broadcasted_iota(jnp.int32, shape, dim)


def params(mib=16):
    return pltpu.CompilerParams(vmem_limit_bytes=mib * 1024 * 1024)


def cost(flops, nbytes):
    return pl.CostEstimate(flops=flops, bytes_accessed=nbytes, transcendentals=0)


def one_hot(row, start, rows):
    line = lax.broadcasted_iota(jnp.int16, (rows, row.shape[1]), 0)
    found = line == (row - start).astype(jnp.int16)
    return jnp.where(found, jnp.ones((), BF16), jnp.zeros((), BF16))


def rows_times(a, b):
    return lax.dot_general(a, b, (((1,), (1,)), ((), ())), preferred_element_type=F32)


def plan_kernel(capacity, nodes, pole, node, slot, pick, where, slot_row):
    slots, blocks = pick.shape
    here = pole[0]
    slot_row[...] = slot[pl.ds(here, 1), :]
    row = node[pl.ds(here, 1), :]
    tile = min(256, blocks)
    earlier = jnp.where(iota((tile, tile), 0) < iota((tile, tile), 1), 1.0, 0.0).astype(BF16)
    seen = jnp.zeros((nodes, 1), F32)
    for start in range(0, blocks, tile):
        part = row[:, start : start + tile]
        same = jnp.where(iota((nodes, tile), 0) == part, 1.0, 0.0)
        before = jnp.dot(same.astype(BF16), earlier, preferred_element_type=F32) + seen
        rank = jnp.sum(same * before, axis=0, keepdims=True).astype(jnp.int32)
        where[:, start : start + tile] = part * capacity + rank
        seen = seen + jnp.sum(same, axis=1, keepdims=True)
    place = where[...]
    for start in range(0, slots, tile):
        pick[start : start + tile, :] = one_hot(place, start, tile)


def deriv_kernel(half, deriv, out_second, out_first):
    rows = deriv.shape[0]
    split = out_second.shape[2]
    wide = split + out_first.shape[2]
    values = deriv[...].astype(F32)
    for c in range(3):
        first = values[:, c * half : (c + 1) * half]
        second = -values[:, (3 + c) * half : (4 + c) * half]
        rest = jnp.zeros((rows, wide - 2 * half), F32)
        line = jnp.concatenate([first, second, rest], axis=1).astype(BF16)
        out_second[c] = line[:, :split]
        out_first[c] = line[:, split:]


def pole_total(parts):
    total = parts[0][...].astype(F32)
    for other in parts[1:]:
        total = total + other[...].astype(F32)
    return total


def pack_first_kernel(pick, slot_row, *refs):
    *parts, out, dens, rows, sem = refs
    columns = parts[0].shape[0]
    wide = dens.shape[0]
    slot = slot_row[...]
    dens[columns:, :] = jnp.zeros((wide - columns, dens.shape[1]), F32)
    dens[:columns, :] = pole_total(parts)
    dens[columns : columns + 1, :] = (slot // BASE + 1).astype(F32)
    dens[columns + 1 : columns + 2, :] = (slot % BASE).astype(F32)
    total = dens[...].astype(BF16)
    tile = min(512, rows.shape[0])
    copies = []
    for start in range(0, rows.shape[0], tile):
        part = pl.ds(start, tile)
        rows[part, :] = rows_times(pick[part, :], total).astype(BF16)
        copies.append(
            pltpu.make_async_copy(rows.at[part, :], out.at[part, :], sem.at[start // tile])
        )
        copies[-1].start()
    for copy in copies:
        copy.wait()


def pack_second_kernel(capacity, core, where, *refs):
    *parts, same, other = refs
    total = pole_total(parts).astype(BF16)
    place = where[...]
    block, rank = place // capacity, place % capacity
    row = block // 2 * capacity + rank
    tile = min(512, same.shape[0])
    for out, whose in ((other, 1 - core[0]), (same, core[0])):
        wanted = jnp.where(block % 2 == whose, row, -1)
        for start in range(0, out.shape[0], tile):
            rows = one_hot(wanted, start, tile)
            out[start : start + tile, :] = rows_times(rows, total).astype(BF16)


def row_terms(dens, deriv, start):
    rows, wide = dens.shape
    ones = jnp.ones((8, LANES), BF16)
    terms = []
    for c in range(3):
        prod = dens * deriv[c, start : start + rows, :].astype(F32)
        folded = prod[:, :LANES]
        for first in range(LANES, wide, LANES):
            folded = folded + prod[:, first : first + LANES]
        terms.append(rows_times(ones, folded.astype(BF16))[0:1, :])
    return terms


def contract_first_kernel(columns, capacity, core, arrived, deriv, atoms, info):
    blocks = atoms.shape[1]
    slots, wide = arrived.shape
    line = iota((8, wide), 0)
    picker = jnp.where((iota((8, wide), 1) == line + columns) & (line < 2), 1.0, 0.0)
    coded = rows_times(picker.astype(BF16), arrived[...])
    slot_row = (coded[0:1, :] - 1.0) * BASE + coded[1:2, :]
    info[...] = jnp.zeros_like(info)
    line = jnp.broadcast_to(slot_row, info.shape)
    ahead = pltpu.roll(line, slots - capacity, 1)
    behind = pltpu.roll(line, capacity, 1)
    swapped = jnp.where(iota(info.shape, 1) % (2 * capacity) < capacity, ahead, behind)
    info[3:4, :] = jnp.where(core[0] == 0, line, swapped)[0:1, :]
    info[4:6, :blocks] = atoms[...].astype(F32)
    slot_row = slot_row.astype(jnp.int32)
    tile = min(256, blocks)
    for start in range(0, blocks, tile):
        dens = jnp.dot(
            one_hot(slot_row, start, tile), arrived[...], preferred_element_type=F32
        )
        for c, term in enumerate(row_terms(dens, deriv, start)):
            info[c : c + 1, start : start + tile] = term


def force_kernel(arrived, source, info, out, total, deriv, sem):
    blocks = deriv.shape[1]
    owners = out.shape[1]
    slot_row = info[3:4, :].astype(jnp.int32)
    tile = min(512, blocks)
    copies = []
    for i in range(blocks // tile):
        rows = pl.ds(i * tile, tile)
        copies.append(
            pltpu.make_async_copy(source.at[:, rows, :], deriv.at[:, rows, :], sem.at[i])
        )
        copies[i].start()
    for start in range(0, blocks, tile):
        dens = jnp.dot(
            one_hot(slot_row, start, tile), arrived[...], preferred_element_type=F32
        )
        copies[start // tile].wait()
        terms = row_terms(dens, deriv, start)
        added = None
        for e, sign in ((0, -2.0), (1, 2.0)):
            atom = info[4 + e : 5 + e, start : start + tile].astype(jnp.int32)
            found = iota((ATOM_DEV, tile), 0) == atom % ATOM_DEV
            weighted = []
            for c in range(3):
                term = sign * (terms[c] + info[c : c + 1, start : start + tile])
                weighted.append(jnp.where(found, term, 0.0).astype(BF16))
            owner = one_hot(atom // ATOM_DEV, 0, owners)
            moved = rows_times(owner, jnp.concatenate(weighted, axis=0))
            added = moved if added is None else added + moved
        if start == 0:
            total[...] = added
        else:
            total[...] += added
    for c in range(3):
        out[c] = total[:, c * ATOM_DEV : (c + 1) * ATOM_DEV].astype(BF16)


def body(dens_part, dest_node, pair_slot, deriv, pair_atoms):
    blocks = deriv.shape[0]
    width = dens_part.shape[2]
    half_width = width // 2
    split = width // LANES * LANES
    last = width - split
    wide = (last + 2 + LANES - 1) // LANES * LANES
    nodes = lax.axis_size("node")
    poles = lax.axis_size("pole")
    pole = lax.axis_index("pole")
    capacity = 2 * blocks // nodes
    slots = nodes * capacity
    owners = poles * nodes
    partials = dens_part[0].T

    def exchange(first_column, columns):
        def share(which):
            start = lax.rem(pole + which, poles) * blocks
            return lax.dynamic_slice(partials, (first_column, start), (columns, blocks))

        parts = []
        for step in (1, 3, 2):
            pairs = [(k, (k + step) % poles) for k in range(poles)]
            parts.append(lax.ppermute(share(step), "pole", pairs))
        return parts

    with jax.named_scope("pole_exchange_first"):
        parts_first = exchange(split, last)
        parts_first.append(
            lax.dynamic_slice(partials, (split, pole * blocks), (last, blocks))
        )
    with jax.named_scope("pole_exchange_second"):
        parts_second = exchange(0, split)

    whole = pl.BlockSpec(memory_space=pltpu.VMEM)
    scalar = pl.BlockSpec(memory_space=pltpu.SMEM)
    pick_out, place, slot_row = pl.pallas_call(
        functools.partial(plan_kernel, capacity, nodes),
        in_specs=[scalar, whole, whole],
        out_shape=[
            jax.ShapeDtypeStruct((slots, blocks), BF16),
            jax.ShapeDtypeStruct((1, blocks), jnp.int32),
            jax.ShapeDtypeStruct((1, blocks), jnp.int32),
        ],
        compiler_params=params(),
        cost_estimate=cost(6 * blocks * blocks, 2 * slots * blocks),
        name="placement",
    )(pole.reshape(1), dest_node.reshape(poles, blocks), pair_slot.reshape(poles, blocks))

    tile = min(256, blocks)
    deriv_second, deriv_first = pl.pallas_call(
        functools.partial(deriv_kernel, half_width),
        grid=(blocks // tile,),
        in_specs=[pl.BlockSpec((tile, deriv.shape[1]), lambda i: (i, 0))],
        out_specs=[
            pl.BlockSpec((3, tile, split), lambda i: (0, i, 0)),
            pl.BlockSpec((3, tile, wide), lambda i: (0, i, 0)),
        ],
        out_shape=[
            pltpu.HBM((3, blocks, split), BF16),
            jax.ShapeDtypeStruct((3, blocks, wide), BF16),
        ],
        compiler_params=params(60),
        cost_estimate=cost(6 * blocks * width, 4 * blocks * deriv.shape[1]),
        name="align_derivatives",
    )(deriv)

    def route(packed):
        columns = packed.shape[1]
        moved = lax.all_to_all(
            packed.reshape(nodes, capacity, columns), "node", 0, 0, tiled=True
        )
        return moved.reshape(slots, columns)

    packed_first = pl.pallas_call(
        pack_first_kernel,
        out_shape=jax.ShapeDtypeStruct((slots, wide), BF16),
        out_specs=pl.BlockSpec(memory_space=pltpu.HBM),
        scratch_shapes=[
            pltpu.VMEM((wide, blocks), F32),
            pltpu.VMEM((slots, wide), BF16),
            pltpu.SemaphoreType.DMA((max(1, slots // 512),)),
        ],
        compiler_params=params(),
        cost_estimate=cost(16 * slots * blocks * wide, 16 * slots * blocks),
        name="pack_first",
    )(pick_out, slot_row, *parts_first)
    with jax.named_scope("pole_exchange_second"):
        later, packed_first = lax.optimization_barrier((partials, packed_first))
        parts_second.append(
            lax.dynamic_slice(later, (0, pole * blocks), (split, blocks))
        )
    with jax.named_scope("route_first"):
        arrived_first = route(packed_first)

    core = lax.rem(lax.axis_index("node"), 2)
    half = jax.ShapeDtypeStruct((slots // 2, split), BF16)
    same_core, other_core = pl.pallas_call(
        functools.partial(pack_second_kernel, capacity),
        in_specs=[scalar] + [whole] * (1 + len(parts_second)),
        out_shape=[half, half],
        compiler_params=params(),
        cost_estimate=cost(200 * slots * blocks * split, 200 * slots * blocks),
        name="pack_second",
    )(core.reshape(1), place, *parts_second)
    with jax.named_scope("route_second"):
        sibling = lax.ppermute(other_core, "node", [(k, k ^ 1) for k in range(nodes)])
        chips = nodes // 2
        both = jnp.concatenate(
            [x.reshape(chips, capacity, split) for x in (same_core, sibling)], axis=1
        )
        groups = [list(range(c, nodes, 2)) for c in range(2)]
        arrived_second = lax.all_to_all(
            both, "node", 0, 0, axis_index_groups=groups, tiled=True
        ).reshape(slots, split)

    info = pl.pallas_call(
        functools.partial(contract_first_kernel, last, capacity),
        in_specs=[scalar, whole, whole, whole],
        out_shape=jax.ShapeDtypeStruct((8, slots), F32),
        compiler_params=params(),
        cost_estimate=cost(2 * slots * blocks * wide, 2 * slots * blocks),
        name="contract_first",
    )(core.reshape(1), arrived_first, deriv_first, pair_atoms)

    partial_forces = pl.pallas_call(
        force_kernel,
        in_specs=[whole, pl.BlockSpec(memory_space=pltpu.HBM), whole],
        out_shape=jax.ShapeDtypeStruct((3, owners, ATOM_DEV), BF16),
        scratch_shapes=[
            pltpu.VMEM((owners, 3 * ATOM_DEV), F32),
            pltpu.VMEM((3, blocks, split), BF16),
            pltpu.SemaphoreType.DMA((max(1, blocks // 512),)),
        ],
        compiler_params=params(),
        cost_estimate=cost(2 * slots * blocks * split, 2 * slots * blocks),
        name="contract_and_scatter",
    )(arrived_second, pltpu.with_memory_space_constraint(deriv_second, pltpu.HBM), info)

    with jax.named_scope("force_exchange"):
        gathered = lax.all_to_all(
            jnp.transpose(partial_forces, (1, 0, 2)), ("pole", "node"), 0, 0, tiled=True
        )
        return jnp.sum(gathered.astype(F32), axis=0)


def solution(mesh):
    return jax.shard_map(
        body,
        mesh=mesh,
        in_specs=(
            P("pole", "node", None),
            P("node"),
            P("node"),
            P(("pole", "node"), None),
            P(None, ("pole", "node")),
        ),
        out_specs=P(None, ("pole", "node")),
        check_vma=False,
    )
```

```python
import functools

import jax
import jax.numpy as jnp
from jax import lax
from jax.experimental import pallas as pl
from jax.experimental.pallas import tpu as pltpu
from jax.sharding import PartitionSpec as P

ATOM_DEV = 128
LANES = 128
BASE = 32
F32 = jnp.float32
BF16 = jnp.bfloat16


def iota(shape, dim):
    return lax.broadcasted_iota(jnp.int32, shape, dim)


def params(mib=16):
    return pltpu.CompilerParams(vmem_limit_bytes=mib * 1024 * 1024)


def cost(flops, nbytes):
    return pl.CostEstimate(flops=flops, bytes_accessed=nbytes, transcendentals=0)


def one_hot(row, start, rows):
    line = lax.broadcasted_iota(jnp.int16, (rows, row.shape[1]), 0)
    found = line == (row - start).astype(jnp.int16)
    return jnp.where(found, jnp.ones((), BF16), jnp.zeros((), BF16))


def rows_times(a, b):
    return lax.dot_general(a, b, (((1,), (1,)), ((), ())), preferred_element_type=F32)


def plan_kernel(capacity, nodes, pole, node, slot, where, slot_row):
    blocks = node.shape[1]
    here = pole[0]
    slot_row[...] = slot[pl.ds(here, 1), :]
    row = node[pl.ds(here, 1), :]
    tile = min(256, blocks)
    earlier = jnp.where(iota((tile, tile), 0) < iota((tile, tile), 1), 1.0, 0.0).astype(BF16)
    seen = jnp.zeros((nodes, 1), F32)
    for start in range(0, blocks, tile):
        part = row[:, start : start + tile]
        same = jnp.where(iota((nodes, tile), 0) == part, 1.0, 0.0)
        before = jnp.dot(same.astype(BF16), earlier, preferred_element_type=F32) + seen
        rank = jnp.sum(same * before, axis=0, keepdims=True).astype(jnp.int32)
        where[:, start : start + tile] = part * capacity + rank
        seen = seen + jnp.sum(same, axis=1, keepdims=True)


def deriv_kernel(half, deriv, out_second, out_first):
    rows = deriv.shape[0]
    split = out_second.shape[2]
    wide = split + out_first.shape[2]
    values = deriv[...].astype(F32)
    for c in range(3):
        first = values[:, c * half : (c + 1) * half]
        second = -values[:, (3 + c) * half : (4 + c) * half]
        rest = jnp.zeros((rows, wide - 2 * half), F32)
        line = jnp.concatenate([first, second, rest], axis=1).astype(BF16)
        out_second[c] = line[:, :split]
        out_first[c] = line[:, split:]


def pole_total(parts):
    total = parts[0][...].astype(F32)
    for other in parts[1:]:
        total = total + other[...].astype(F32)
    return total


def pack_first_kernel(where, slot_row, *refs):
    *parts, out, dens, rows, sem = refs
    columns = parts[0].shape[0]
    wide = dens.shape[0]
    slot = slot_row[...]
    dens[columns:, :] = jnp.zeros((wide - columns, dens.shape[1]), F32)
    dens[:columns, :] = pole_total(parts)
    dens[columns : columns + 1, :] = (slot // BASE + 1).astype(F32)
    dens[columns + 1 : columns + 2, :] = (slot % BASE).astype(F32)
    total = dens[...].astype(BF16)
    tile = min(512, rows.shape[0])
    copies = []
    place = where[...]
    for start in range(0, rows.shape[0], tile):
        part = pl.ds(start, tile)
        picked = one_hot(place, start, tile)
        rows[part, :] = rows_times(picked, total).astype(BF16)
        copies.append(
            pltpu.make_async_copy(rows.at[part, :], out.at[part, :], sem.at[start // tile])
        )
        copies[-1].start()
    for copy in copies:
        copy.wait()


def pack_second_kernel(capacity, core, where, *refs):
    *parts, same, other = refs
    total = pole_total(parts).astype(BF16)
    place = where[...]
    block, rank = place // capacity, place % capacity
    row = block // 2 * capacity + rank
    tile = min(512, same.shape[0])
    for out, whose in ((other, 1 - core[0]), (same, core[0])):
        wanted = jnp.where(block % 2 == whose, row, -1)
        for start in range(0, out.shape[0], tile):
            rows = one_hot(wanted, start, tile)
            out[start : start + tile, :] = rows_times(rows, total).astype(BF16)


def row_terms(dens, deriv, start):
    rows, wide = dens.shape
    ones = jnp.ones((8, LANES), BF16)
    terms = []
    for c in range(3):
        prod = dens * deriv[c, start : start + rows, :].astype(F32)
        folded = prod[:, :LANES]
        for first in range(LANES, wide, LANES):
            folded = folded + prod[:, first : first + LANES]
        terms.append(rows_times(ones, folded.astype(BF16))[0:1, :])
    return terms


def contract_first_kernel(columns, capacity, core, arrived, deriv, atoms, info):
    blocks = atoms.shape[1]
    slots, wide = arrived.shape
    line = iota((8, wide), 0)
    picker = jnp.where((iota((8, wide), 1) == line + columns) & (line < 2), 1.0, 0.0)
    coded = rows_times(picker.astype(BF16), arrived[...])
    slot_row = (coded[0:1, :] - 1.0) * BASE + coded[1:2, :]
    info[...] = jnp.zeros_like(info)
    line = jnp.broadcast_to(slot_row, info.shape)
    ahead = pltpu.roll(line, slots - capacity, 1)
    behind = pltpu.roll(line, capacity, 1)
    swapped = jnp.where(iota(info.shape, 1) % (2 * capacity) < capacity, ahead, behind)
    info[3:4, :] = jnp.where(core[0] == 0, line, swapped)[0:1, :]
    info[4:6, :blocks] = atoms[...].astype(F32)
    slot_row = slot_row.astype(jnp.int32)
    tile = min(256, blocks)
    for start in range(0, blocks, tile):
        dens = jnp.dot(
            one_hot(slot_row, start, tile), arrived[...], preferred_element_type=F32
        )
        for c, term in enumerate(row_terms(dens, deriv, start)):
            info[c : c + 1, start : start + tile] = term


def force_kernel(arrived, source, info, out, total, deriv, sem):
    blocks = deriv.shape[1]
    owners = out.shape[1]
    slot_row = info[3:4, :].astype(jnp.int32)
    tile = min(512, blocks)
    copies = []
    for i in range(blocks // tile):
        rows = pl.ds(i * tile, tile)
        copies.append(
            pltpu.make_async_copy(source.at[:, rows, :], deriv.at[:, rows, :], sem.at[i])
        )
        copies[i].start()
    for start in range(0, blocks, tile):
        dens = jnp.dot(
            one_hot(slot_row, start, tile), arrived[...], preferred_element_type=F32
        )
        copies[start // tile].wait()
        terms = row_terms(dens, deriv, start)
        added = None
        for e, sign in ((0, -2.0), (1, 2.0)):
            atom = info[4 + e : 5 + e, start : start + tile].astype(jnp.int32)
            found = iota((ATOM_DEV, tile), 0) == atom % ATOM_DEV
            weighted = []
            for c in range(3):
                term = sign * (terms[c] + info[c : c + 1, start : start + tile])
                weighted.append(jnp.where(found, term, 0.0).astype(BF16))
            owner = one_hot(atom // ATOM_DEV, 0, owners)
            moved = rows_times(owner, jnp.concatenate(weighted, axis=0))
            added = moved if added is None else added + moved
        if start == 0:
            total[...] = added
        else:
            total[...] += added
    for c in range(3):
        out[c] = total[:, c * ATOM_DEV : (c + 1) * ATOM_DEV].astype(BF16)


def body(dens_part, dest_node, pair_slot, deriv, pair_atoms):
    blocks = deriv.shape[0]
    width = dens_part.shape[2]
    half_width = width // 2
    split = width // LANES * LANES
    last = width - split
    wide = (last + 2 + LANES - 1) // LANES * LANES
    nodes = lax.axis_size("node")
    poles = lax.axis_size("pole")
    pole = lax.axis_index("pole")
    capacity = 2 * blocks // nodes
    slots = nodes * capacity
    owners = poles * nodes
    partials = dens_part[0].T

    def exchange(first_column, columns, steps):
        def share(which):
            start = lax.rem(pole + which, poles) * blocks
            return lax.dynamic_slice(partials, (first_column, start), (columns, blocks))

        parts = []
        for step in steps:
            pairs = [(k, (k + step) % poles) for k in range(poles)]
            parts.append(lax.ppermute(share(step), "pole", pairs))
        return parts

    with jax.named_scope("pole_exchange_first"):
        parts_first = exchange(split, last, (2, 1, 3))
        parts_first.append(
            lax.dynamic_slice(partials, (split, pole * blocks), (last, blocks))
        )
    with jax.named_scope("pole_exchange_second"):
        parts_second = exchange(0, split, (1, 3, 2))

    whole = pl.BlockSpec(memory_space=pltpu.VMEM)
    scalar = pl.BlockSpec(memory_space=pltpu.SMEM)
    place, slot_row = pl.pallas_call(
        functools.partial(plan_kernel, capacity, nodes),
        in_specs=[scalar, whole, whole],
        out_shape=[
            jax.ShapeDtypeStruct((1, blocks), jnp.int32),
            jax.ShapeDtypeStruct((1, blocks), jnp.int32),
        ],
        compiler_params=params(),
        cost_estimate=cost(6 * blocks * blocks, 2 * slots * blocks),
        name="placement",
    )(pole.reshape(1), dest_node.reshape(poles, blocks), pair_slot.reshape(poles, blocks))

    tile = min(256, blocks)
    deriv_second, deriv_first = pl.pallas_call(
        functools.partial(deriv_kernel, half_width),
        grid=(blocks // tile,),
        in_specs=[pl.BlockSpec((tile, deriv.shape[1]), lambda i: (i, 0))],
        out_specs=[
            pl.BlockSpec((3, tile, split), lambda i: (0, i, 0)),
            pl.BlockSpec((3, tile, wide), lambda i: (0, i, 0)),
        ],
        out_shape=[
            pltpu.HBM((3, blocks, split), BF16),
            jax.ShapeDtypeStruct((3, blocks, wide), BF16),
        ],
        compiler_params=params(60),
        cost_estimate=cost(6 * blocks * width, 4 * blocks * deriv.shape[1]),
        name="align_derivatives",
    )(deriv)

    def route(packed):
        columns = packed.shape[1]
        moved = lax.all_to_all(
            packed.reshape(nodes, capacity, columns), "node", 0, 0, tiled=True
        )
        return moved.reshape(slots, columns)

    packed_first = pl.pallas_call(
        pack_first_kernel,
        out_shape=jax.ShapeDtypeStruct((slots, wide), BF16),
        out_specs=pl.BlockSpec(memory_space=pltpu.HBM),
        scratch_shapes=[
            pltpu.VMEM((wide, blocks), F32),
            pltpu.VMEM((slots, wide), BF16),
            pltpu.SemaphoreType.DMA((max(1, slots // 512),)),
        ],
        compiler_params=params(),
        cost_estimate=cost(16 * slots * blocks * wide, 16 * slots * blocks),
        name="pack_first",
    )(place, slot_row, *parts_first)
    with jax.named_scope("pole_exchange_second"):
        later, packed_first = lax.optimization_barrier((partials, packed_first))
        parts_second.append(
            lax.dynamic_slice(later, (0, pole * blocks), (split, blocks))
        )
    with jax.named_scope("route_first"):
        arrived_first = route(packed_first)

    core = lax.rem(lax.axis_index("node"), 2)
    half = jax.ShapeDtypeStruct((slots // 2, split), BF16)
    same_core, other_core = pl.pallas_call(
        functools.partial(pack_second_kernel, capacity),
        in_specs=[scalar] + [whole] * (1 + len(parts_second)),
        out_shape=[half, half],
        compiler_params=params(),
        cost_estimate=cost(200 * slots * blocks * split, 200 * slots * blocks),
        name="pack_second",
    )(core.reshape(1), place, *parts_second)
    with jax.named_scope("route_second"):
        sibling = lax.ppermute(other_core, "node", [(k, k ^ 1) for k in range(nodes)])
        chips = nodes // 2
        both = jnp.concatenate(
            [x.reshape(chips, capacity, split) for x in (same_core, sibling)], axis=1
        )
        groups = [list(range(c, nodes, 2)) for c in range(2)]
        arrived_second = lax.all_to_all(
            both, "node", 0, 0, axis_index_groups=groups, tiled=True
        ).reshape(slots, split)

    info = pl.pallas_call(
        functools.partial(contract_first_kernel, last, capacity),
        in_specs=[scalar, whole, whole, whole],
        out_shape=jax.ShapeDtypeStruct((8, slots), F32),
        compiler_params=params(),
        cost_estimate=cost(2 * slots * blocks * wide, 2 * slots * blocks),
        name="contract_first",
    )(core.reshape(1), arrived_first, deriv_first, pair_atoms)

    partial_forces = pl.pallas_call(
        force_kernel,
        in_specs=[whole, pl.BlockSpec(memory_space=pltpu.HBM), whole],
        out_shape=jax.ShapeDtypeStruct((3, owners, ATOM_DEV), BF16),
        scratch_shapes=[
            pltpu.VMEM((owners, 3 * ATOM_DEV), F32),
            pltpu.VMEM((3, blocks, split), BF16),
            pltpu.SemaphoreType.DMA((max(1, blocks // 512),)),
        ],
        compiler_params=params(),
        cost_estimate=cost(2 * slots * blocks * split, 2 * slots * blocks),
        name="contract_and_scatter",
    )(arrived_second, pltpu.with_memory_space_constraint(deriv_second, pltpu.HBM), info)

    with jax.named_scope("force_exchange"):
        gathered = lax.all_to_all(
            jnp.transpose(partial_forces, (1, 0, 2)), ("pole", "node"), 0, 0, tiled=True
        )
        return jnp.sum(gathered.astype(F32), axis=0)


def solution(mesh):
    return jax.shard_map(
        body,
        mesh=mesh,
        in_specs=(
            P("pole", "node", None),
            P("node"),
            P("node"),
            P(("pole", "node"), None),
            P(None, ("pole", "node")),
        ),
        out_specs=P(None, ("pole", "node")),
        check_vma=False,
    )
```

```python
import functools

import jax
import jax.numpy as jnp
from jax import lax
from jax.experimental import pallas as pl
from jax.experimental.pallas import tpu as pltpu
from jax.sharding import PartitionSpec as P

ATOM_DEV = 128
LANES = 128
BASE = 32
F32 = jnp.float32
BF16 = jnp.bfloat16


def iota(shape, dim):
    return lax.broadcasted_iota(jnp.int32, shape, dim)


def params(mib=16):
    return pltpu.CompilerParams(vmem_limit_bytes=mib * 1024 * 1024)


def cost(flops, nbytes):
    return pl.CostEstimate(flops=flops, bytes_accessed=nbytes, transcendentals=0)


def one_hot(row, start, rows):
    line = lax.broadcasted_iota(jnp.int16, (rows, row.shape[1]), 0)
    found = line == (row - start).astype(jnp.int16)
    return jnp.where(found, jnp.ones((), BF16), jnp.zeros((), BF16))


def rows_times(a, b):
    return lax.dot_general(a, b, (((1,), (1,)), ((), ())), preferred_element_type=F32)


def plan_kernel(capacity, nodes, pole, node, slot, pick, where, slot_row):
    slots, blocks = pick.shape
    here = pole[0]
    slot_row[...] = slot[pl.ds(here, 1), :]
    row = node[pl.ds(here, 1), :]
    tile = min(256, blocks)
    earlier = jnp.where(iota((tile, tile), 0) < iota((tile, tile), 1), 1.0, 0.0).astype(BF16)
    seen = jnp.zeros((nodes, 1), F32)
    for start in range(0, blocks, tile):
        part = row[:, start : start + tile]
        same = jnp.where(iota((nodes, tile), 0) == part, 1.0, 0.0)
        before = jnp.dot(same.astype(BF16), earlier, preferred_element_type=F32) + seen
        rank = jnp.sum(same * before, axis=0, keepdims=True).astype(jnp.int32)
        where[:, start : start + tile] = part * capacity + rank
        seen = seen + jnp.sum(same, axis=1, keepdims=True)
    place = where[...]
    for start in range(0, slots, tile):
        pick[start : start + tile, :] = one_hot(place, start, tile)


def deriv_kernel(half, deriv, out_second, out_first):
    rows = deriv.shape[0]
    split = out_second.shape[2]
    wide = split + out_first.shape[2]
    values = deriv[...].astype(F32)
    for c in range(3):
        first = values[:, c * half : (c + 1) * half]
        second = -values[:, (3 + c) * half : (4 + c) * half]
        rest = jnp.zeros((rows, wide - 2 * half), F32)
        line = jnp.concatenate([first, second, rest], axis=1).astype(BF16)
        out_second[c] = line[:, :split]
        out_first[c] = line[:, split:]


def pole_total(parts):
    total = parts[0][...].astype(F32)
    for other in parts[1:]:
        total = total + other[...].astype(F32)
    return total


def pack_first_kernel(pick, slot_row, *refs):
    *parts, out, dens, rows, sem = refs
    columns = parts[0].shape[0]
    wide = dens.shape[0]
    slot = slot_row[...]
    dens[columns:, :] = jnp.zeros((wide - columns, dens.shape[1]), F32)
    dens[:columns, :] = pole_total(parts)
    dens[columns : columns + 1, :] = (slot // BASE + 1).astype(F32)
    dens[columns + 1 : columns + 2, :] = (slot % BASE).astype(F32)
    total = dens[...].astype(BF16)
    tile = min(256, rows.shape[0])
    copies = []
    for start in range(0, rows.shape[0], tile):
        part = pl.ds(start, tile)
        rows[part, :] = rows_times(pick[part, :], total).astype(BF16)
        copies.append(
            pltpu.make_async_copy(rows.at[part, :], out.at[part, :], sem.at[start // tile])
        )
        copies[-1].start()
    for copy in copies:
        copy.wait()


def pack_second_kernel(capacity, core, where, *refs):
    *parts, same, other = refs
    total = pole_total(parts).astype(BF16)
    place = where[...]
    block, rank = place // capacity, place % capacity
    row = block // 2 * capacity + rank
    tile = min(512, same.shape[0])
    for out, whose in ((other, 1 - core[0]), (same, core[0])):
        wanted = jnp.where(block % 2 == whose, row, -1)
        for start in range(0, out.shape[0], tile):
            rows = one_hot(wanted, start, tile)
            out[start : start + tile, :] = rows_times(rows, total).astype(BF16)


def row_terms(dens, deriv, start):
    rows, wide = dens.shape
    ones = jnp.ones((8, LANES), BF16)
    terms = []
    for c in range(3):
        prod = dens * deriv[c, start : start + rows, :].astype(F32)
        folded = prod[:, :LANES]
        for first in range(LANES, wide, LANES):
            folded = folded + prod[:, first : first + LANES]
        terms.append(rows_times(ones, folded.astype(BF16))[0:1, :])
    return terms


def contract_first_kernel(columns, capacity, core, arrived, deriv, atoms, info):
    blocks = atoms.shape[1]
    slots, wide = arrived.shape
    line = iota((8, wide), 0)
    picker = jnp.where((iota((8, wide), 1) == line + columns) & (line < 2), 1.0, 0.0)
    coded = rows_times(picker.astype(BF16), arrived[...])
    slot_row = (coded[0:1, :] - 1.0) * BASE + coded[1:2, :]
    info[...] = jnp.zeros_like(info)
    line = jnp.broadcast_to(slot_row, info.shape)
    ahead = pltpu.roll(line, slots - capacity, 1)
    behind = pltpu.roll(line, capacity, 1)
    swapped = jnp.where(iota(info.shape, 1) % (2 * capacity) < capacity, ahead, behind)
    info[3:4, :] = jnp.where(core[0] == 0, line, swapped)[0:1, :]
    info[4:6, :blocks] = atoms[...].astype(F32)
    slot_row = slot_row.astype(jnp.int32)
    tile = min(256, blocks)
    for start in range(0, blocks, tile):
        dens = jnp.dot(
            one_hot(slot_row, start, tile), arrived[...], preferred_element_type=F32
        )
        for c, term in enumerate(row_terms(dens, deriv, start)):
            info[c : c + 1, start : start + tile] = term


def force_kernel(arrived, source, info, out, total, deriv, sem):
    blocks = deriv.shape[1]
    owners = out.shape[1]
    slot_row = info[3:4, :].astype(jnp.int32)
    tile = min(512, blocks)
    copies = []
    for i in range(blocks // tile):
        rows = pl.ds(i * tile, tile)
        copies.append(
            pltpu.make_async_copy(source.at[:, rows, :], deriv.at[:, rows, :], sem.at[i])
        )
        copies[i].start()
    for start in range(0, blocks, tile):
        dens = jnp.dot(
            one_hot(slot_row, start, tile), arrived[...], preferred_element_type=F32
        )
        copies[start // tile].wait()
        terms = row_terms(dens, deriv, start)
        added = None
        for e, sign in ((0, -2.0), (1, 2.0)):
            atom = info[4 + e : 5 + e, start : start + tile].astype(jnp.int32)
            found = iota((ATOM_DEV, tile), 0) == atom % ATOM_DEV
            weighted = []
            for c in range(3):
                term = sign * (terms[c] + info[c : c + 1, start : start + tile])
                weighted.append(jnp.where(found, term, 0.0).astype(BF16))
            owner = one_hot(atom // ATOM_DEV, 0, owners)
            moved = rows_times(owner, jnp.concatenate(weighted, axis=0))
            added = moved if added is None else added + moved
        if start == 0:
            total[...] = added
        else:
            total[...] += added
    for c in range(3):
        out[c] = total[:, c * ATOM_DEV : (c + 1) * ATOM_DEV].astype(BF16)


def body(dens_part, dest_node, pair_slot, deriv, pair_atoms):
    blocks = deriv.shape[0]
    width = dens_part.shape[2]
    half_width = width // 2
    split = width // LANES * LANES
    last = width - split
    wide = (last + 2 + LANES - 1) // LANES * LANES
    nodes = lax.axis_size("node")
    poles = lax.axis_size("pole")
    pole = lax.axis_index("pole")
    capacity = 2 * blocks // nodes
    slots = nodes * capacity
    owners = poles * nodes
    partials = dens_part[0].T

    def exchange(first_column, columns):
        def share(which):
            start = lax.rem(pole + which, poles) * blocks
            return lax.dynamic_slice(partials, (first_column, start), (columns, blocks))

        parts = []
        for step in (1, 3, 2):
            pairs = [(k, (k + step) % poles) for k in range(poles)]
            parts.append(lax.ppermute(share(step), "pole", pairs))
        return parts

    with jax.named_scope("pole_exchange_first"):
        parts_first = exchange(split, last)
        parts_first.append(
            lax.dynamic_slice(partials, (split, pole * blocks), (last, blocks))
        )
    with jax.named_scope("pole_exchange_second"):
        parts_second = exchange(0, split)

    whole = pl.BlockSpec(memory_space=pltpu.VMEM)
    scalar = pl.BlockSpec(memory_space=pltpu.SMEM)
    pick_out, place, slot_row = pl.pallas_call(
        functools.partial(plan_kernel, capacity, nodes),
        in_specs=[scalar, whole, whole],
        out_shape=[
            jax.ShapeDtypeStruct((slots, blocks), BF16),
            jax.ShapeDtypeStruct((1, blocks), jnp.int32),
            jax.ShapeDtypeStruct((1, blocks), jnp.int32),
        ],
        compiler_params=params(),
        cost_estimate=cost(6 * blocks * blocks, 2 * slots * blocks),
        name="placement",
    )(pole.reshape(1), dest_node.reshape(poles, blocks), pair_slot.reshape(poles, blocks))

    tile = min(256, blocks)
    deriv_second, deriv_first = pl.pallas_call(
        functools.partial(deriv_kernel, half_width),
        grid=(blocks // tile,),
        in_specs=[pl.BlockSpec((tile, deriv.shape[1]), lambda i: (i, 0))],
        out_specs=[
            pl.BlockSpec((3, tile, split), lambda i: (0, i, 0)),
            pl.BlockSpec((3, tile, wide), lambda i: (0, i, 0)),
        ],
        out_shape=[
            pltpu.HBM((3, blocks, split), BF16),
            jax.ShapeDtypeStruct((3, blocks, wide), BF16),
        ],
        compiler_params=params(60),
        cost_estimate=cost(6 * blocks * width, 4 * blocks * deriv.shape[1]),
        name="align_derivatives",
    )(deriv)

    def route(packed):
        columns = packed.shape[1]
        moved = lax.all_to_all(
            packed.reshape(nodes, capacity, columns), "node", 0, 0, tiled=True
        )
        return moved.reshape(slots, columns)

    packed_first = pl.pallas_call(
        pack_first_kernel,
        out_shape=jax.ShapeDtypeStruct((slots, wide), BF16),
        out_specs=pl.BlockSpec(memory_space=pltpu.HBM),
        scratch_shapes=[
            pltpu.VMEM((wide, blocks), F32),
            pltpu.VMEM((slots, wide), BF16),
            pltpu.SemaphoreType.DMA((max(1, slots // 256),)),
        ],
        compiler_params=params(),
        cost_estimate=cost(16 * slots * blocks * wide, 16 * slots * blocks),
        name="pack_first",
    )(pick_out, slot_row, *parts_first)
    with jax.named_scope("pole_exchange_second"):
        later, packed_first = lax.optimization_barrier((partials, packed_first))
        parts_second.append(
            lax.dynamic_slice(later, (0, pole * blocks), (split, blocks))
        )
    with jax.named_scope("route_first"):
        arrived_first = route(packed_first)

    core = lax.rem(lax.axis_index("node"), 2)
    half = jax.ShapeDtypeStruct((slots // 2, split), BF16)
    same_core, other_core = pl.pallas_call(
        functools.partial(pack_second_kernel, capacity),
        in_specs=[scalar] + [whole] * (1 + len(parts_second)),
        out_shape=[half, half],
        compiler_params=params(),
        cost_estimate=cost(200 * slots * blocks * split, 200 * slots * blocks),
        name="pack_second",
    )(core.reshape(1), place, *parts_second)
    with jax.named_scope("route_second"):
        sibling = lax.ppermute(other_core, "node", [(k, k ^ 1) for k in range(nodes)])
        chips = nodes // 2
        both = jnp.concatenate(
            [x.reshape(chips, capacity, split) for x in (same_core, sibling)], axis=1
        )
        groups = [list(range(c, nodes, 2)) for c in range(2)]
        arrived_second = lax.all_to_all(
            both, "node", 0, 0, axis_index_groups=groups, tiled=True
        ).reshape(slots, split)

    info = pl.pallas_call(
        functools.partial(contract_first_kernel, last, capacity),
        in_specs=[scalar, whole, whole, whole],
        out_shape=jax.ShapeDtypeStruct((8, slots), F32),
        compiler_params=params(),
        cost_estimate=cost(2 * slots * blocks * wide, 2 * slots * blocks),
        name="contract_first",
    )(core.reshape(1), arrived_first, deriv_first, pair_atoms)

    partial_forces = pl.pallas_call(
        force_kernel,
        in_specs=[whole, pl.BlockSpec(memory_space=pltpu.HBM), whole],
        out_shape=jax.ShapeDtypeStruct((3, owners, ATOM_DEV), BF16),
        scratch_shapes=[
            pltpu.VMEM((owners, 3 * ATOM_DEV), F32),
            pltpu.VMEM((3, blocks, split), BF16),
            pltpu.SemaphoreType.DMA((max(1, blocks // 512),)),
        ],
        compiler_params=params(),
        cost_estimate=cost(2 * slots * blocks * split, 2 * slots * blocks),
        name="contract_and_scatter",
    )(arrived_second, pltpu.with_memory_space_constraint(deriv_second, pltpu.HBM), info)

    with jax.named_scope("force_exchange"):
        gathered = lax.all_to_all(
            jnp.transpose(partial_forces, (1, 0, 2)), ("pole", "node"), 0, 0, tiled=True
        )
        return jnp.sum(gathered.astype(F32), axis=0)


def solution(mesh):
    return jax.shard_map(
        body,
        mesh=mesh,
        in_specs=(
            P("pole", "node", None),
            P("node"),
            P("node"),
            P(("pole", "node"), None),
            P(None, ("pole", "node")),
        ),
        out_specs=P(None, ("pole", "node")),
        check_vma=False,
    )
```

```python
import functools

import jax
import jax.numpy as jnp
from jax import lax
from jax.experimental import pallas as pl
from jax.experimental.pallas import tpu as pltpu
from jax.sharding import PartitionSpec as P

ATOM_DEV = 128
LANES = 128
BASE = 32
F32 = jnp.float32
BF16 = jnp.bfloat16


def iota(shape, dim):
    return lax.broadcasted_iota(jnp.int32, shape, dim)


def params(mib=16):
    return pltpu.CompilerParams(vmem_limit_bytes=mib * 1024 * 1024)


def cost(flops, nbytes):
    return pl.CostEstimate(flops=flops, bytes_accessed=nbytes, transcendentals=0)


def one_hot(row, start, rows):
    line = lax.broadcasted_iota(jnp.int16, (rows, row.shape[1]), 0)
    found = line == (row - start).astype(jnp.int16)
    return jnp.where(found, jnp.ones((), BF16), jnp.zeros((), BF16))


def rows_times(a, b):
    return lax.dot_general(a, b, (((1,), (1,)), ((), ())), preferred_element_type=F32)


def plan_kernel(capacity, nodes, pole, node, slot, where, slot_row):
    blocks = node.shape[1]
    here = pole[0]
    slot_row[...] = slot[pl.ds(here, 1), :]
    row = node[pl.ds(here, 1), :]
    tile = min(256, blocks)
    earlier = jnp.where(iota((tile, tile), 0) < iota((tile, tile), 1), 1.0, 0.0).astype(BF16)
    seen = jnp.zeros((nodes, 1), F32)
    for start in range(0, blocks, tile):
        part = row[:, start : start + tile]
        same = jnp.where(iota((nodes, tile), 0) == part, 1.0, 0.0)
        before = jnp.dot(same.astype(BF16), earlier, preferred_element_type=F32) + seen
        rank = jnp.sum(same * before, axis=0, keepdims=True).astype(jnp.int32)
        where[:, start : start + tile] = part * capacity + rank
        seen = seen + jnp.sum(same, axis=1, keepdims=True)


def deriv_kernel(half, deriv, out_second, out_first):
    rows = deriv.shape[0]
    split = out_second.shape[2]
    wide = split + out_first.shape[2]
    values = deriv[...].astype(F32)
    for c in range(3):
        first = values[:, c * half : (c + 1) * half]
        second = -values[:, (3 + c) * half : (4 + c) * half]
        rest = jnp.zeros((rows, wide - 2 * half), F32)
        line = jnp.concatenate([first, second, rest], axis=1).astype(BF16)
        out_second[c] = line[:, :split]
        out_first[c] = line[:, split:]


def pole_total(parts):
    total = parts[0][...].astype(F32)
    for other in parts[1:]:
        total = total + other[...].astype(F32)
    return total


def pack_first_kernel(where, slot_row, *refs):
    *parts, out, dens, rows, sem = refs
    columns = parts[0].shape[0]
    wide = dens.shape[0]
    slot = slot_row[...]
    dens[columns:, :] = jnp.zeros((wide - columns, dens.shape[1]), F32)
    dens[:columns, :] = pole_total(parts)
    dens[columns : columns + 1, :] = (slot // BASE + 1).astype(F32)
    dens[columns + 1 : columns + 2, :] = (slot % BASE).astype(F32)
    total = dens[...].astype(BF16)
    tile = min(256, rows.shape[0])
    copies = []
    place = where[...]
    for start in range(0, rows.shape[0], tile):
        part = pl.ds(start, tile)
        picked = one_hot(place, start, tile)
        rows[part, :] = rows_times(picked, total).astype(BF16)
        copies.append(
            pltpu.make_async_copy(rows.at[part, :], out.at[part, :], sem.at[start // tile])
        )
        copies[-1].start()
    for copy in copies:
        copy.wait()


def pack_second_kernel(capacity, core, where, *refs):
    *parts, same, other = refs
    total = pole_total(parts).astype(BF16)
    place = where[...]
    block, rank = place // capacity, place % capacity
    row = block // 2 * capacity + rank
    tile = min(512, same.shape[0])
    for out, whose in ((other, 1 - core[0]), (same, core[0])):
        wanted = jnp.where(block % 2 == whose, row, -1)
        for start in range(0, out.shape[0], tile):
            rows = one_hot(wanted, start, tile)
            out[start : start + tile, :] = rows_times(rows, total).astype(BF16)


def row_terms(dens, deriv, start):
    rows, wide = dens.shape
    ones = jnp.ones((8, LANES), BF16)
    terms = []
    for c in range(3):
        prod = dens * deriv[c, start : start + rows, :].astype(F32)
        folded = prod[:, :LANES]
        for first in range(LANES, wide, LANES):
            folded = folded + prod[:, first : first + LANES]
        terms.append(rows_times(ones, folded.astype(BF16))[0:1, :])
    return terms


def contract_first_kernel(columns, capacity, core, arrived, deriv, atoms, info):
    blocks = atoms.shape[1]
    slots, wide = arrived.shape
    line = iota((8, wide), 0)
    picker = jnp.where((iota((8, wide), 1) == line + columns) & (line < 2), 1.0, 0.0)
    coded = rows_times(picker.astype(BF16), arrived[...])
    slot_row = (coded[0:1, :] - 1.0) * BASE + coded[1:2, :]
    info[...] = jnp.zeros_like(info)
    line = jnp.broadcast_to(slot_row, info.shape)
    ahead = pltpu.roll(line, slots - capacity, 1)
    behind = pltpu.roll(line, capacity, 1)
    swapped = jnp.where(iota(info.shape, 1) % (2 * capacity) < capacity, ahead, behind)
    info[3:4, :] = jnp.where(core[0] == 0, line, swapped)[0:1, :]
    info[4:6, :blocks] = atoms[...].astype(F32)
    slot_row = slot_row.astype(jnp.int32)
    tile = min(256, blocks)
    for start in range(0, blocks, tile):
        dens = jnp.dot(
            one_hot(slot_row, start, tile), arrived[...], preferred_element_type=F32
        )
        for c, term in enumerate(row_terms(dens, deriv, start)):
            info[c : c + 1, start : start + tile] = term


def force_kernel(arrived, source, info, out, total, deriv, sem):
    blocks = deriv.shape[1]
    owners = out.shape[1]
    slot_row = info[3:4, :].astype(jnp.int32)
    tile = min(512, blocks)
    copies = []
    for i in range(blocks // tile):
        rows = pl.ds(i * tile, tile)
        copies.append(
            pltpu.make_async_copy(source.at[:, rows, :], deriv.at[:, rows, :], sem.at[i])
        )
        copies[i].start()
    for start in range(0, blocks, tile):
        dens = jnp.dot(
            one_hot(slot_row, start, tile), arrived[...], preferred_element_type=F32
        )
        copies[start // tile].wait()
        terms = row_terms(dens, deriv, start)
        added = None
        for e, sign in ((0, -2.0), (1, 2.0)):
            atom = info[4 + e : 5 + e, start : start + tile].astype(jnp.int32)
            found = iota((ATOM_DEV, tile), 0) == atom % ATOM_DEV
            weighted = []
            for c in range(3):
                term = sign * (terms[c] + info[c : c + 1, start : start + tile])
                weighted.append(jnp.where(found, term, 0.0).astype(BF16))
            owner = one_hot(atom // ATOM_DEV, 0, owners)
            moved = rows_times(owner, jnp.concatenate(weighted, axis=0))
            added = moved if added is None else added + moved
        if start == 0:
            total[...] = added
        else:
            total[...] += added
    for c in range(3):
        out[c] = total[:, c * ATOM_DEV : (c + 1) * ATOM_DEV].astype(BF16)


def body(dens_part, dest_node, pair_slot, deriv, pair_atoms):
    blocks = deriv.shape[0]
    width = dens_part.shape[2]
    half_width = width // 2
    split = width // LANES * LANES
    last = width - split
    wide = (last + 2 + LANES - 1) // LANES * LANES
    nodes = lax.axis_size("node")
    poles = lax.axis_size("pole")
    pole = lax.axis_index("pole")
    capacity = 2 * blocks // nodes
    slots = nodes * capacity
    owners = poles * nodes
    partials = dens_part[0].T

    def exchange(first_column, columns, steps):
        def share(which):
            start = lax.rem(pole + which, poles) * blocks
            return lax.dynamic_slice(partials, (first_column, start), (columns, blocks))

        parts = []
        for step in steps:
            pairs = [(k, (k + step) % poles) for k in range(poles)]
            parts.append(lax.ppermute(share(step), "pole", pairs))
        return parts

    with jax.named_scope("pole_exchange_first"):
        parts_first = exchange(split, last, (2, 1, 3))
        parts_first.append(
            lax.dynamic_slice(partials, (split, pole * blocks), (last, blocks))
        )
    with jax.named_scope("pole_exchange_second"):
        parts_second = exchange(0, split, (1, 3, 2))

    whole = pl.BlockSpec(memory_space=pltpu.VMEM)
    scalar = pl.BlockSpec(memory_space=pltpu.SMEM)
    place, slot_row = pl.pallas_call(
        functools.partial(plan_kernel, capacity, nodes),
        in_specs=[scalar, whole, whole],
        out_shape=[
            jax.ShapeDtypeStruct((1, blocks), jnp.int32),
            jax.ShapeDtypeStruct((1, blocks), jnp.int32),
        ],
        compiler_params=params(),
        cost_estimate=cost(6 * blocks * blocks, 2 * slots * blocks),
        name="placement",
    )(pole.reshape(1), dest_node.reshape(poles, blocks), pair_slot.reshape(poles, blocks))

    tile = min(256, blocks)
    deriv_second, deriv_first = pl.pallas_call(
        functools.partial(deriv_kernel, half_width),
        grid=(blocks // tile,),
        in_specs=[pl.BlockSpec((tile, deriv.shape[1]), lambda i: (i, 0))],
        out_specs=[
            pl.BlockSpec((3, tile, split), lambda i: (0, i, 0)),
            pl.BlockSpec((3, tile, wide), lambda i: (0, i, 0)),
        ],
        out_shape=[
            pltpu.HBM((3, blocks, split), BF16),
            jax.ShapeDtypeStruct((3, blocks, wide), BF16),
        ],
        compiler_params=params(60),
        cost_estimate=cost(6 * blocks * width, 4 * blocks * deriv.shape[1]),
        name="align_derivatives",
    )(deriv)

    def route(packed):
        columns = packed.shape[1]
        moved = lax.all_to_all(
            packed.reshape(nodes, capacity, columns), "node", 0, 0, tiled=True
        )
        return moved.reshape(slots, columns)

    packed_first = pl.pallas_call(
        pack_first_kernel,
        out_shape=jax.ShapeDtypeStruct((slots, wide), BF16),
        out_specs=pl.BlockSpec(memory_space=pltpu.HBM),
        scratch_shapes=[
            pltpu.VMEM((wide, blocks), F32),
            pltpu.VMEM((slots, wide), BF16),
            pltpu.SemaphoreType.DMA((max(1, slots // 256),)),
        ],
        compiler_params=params(),
        cost_estimate=cost(16 * slots * blocks * wide, 16 * slots * blocks),
        name="pack_first",
    )(place, slot_row, *parts_first)
    with jax.named_scope("pole_exchange_second"):
        later, packed_first = lax.optimization_barrier((partials, packed_first))
        parts_second.append(
            lax.dynamic_slice(later, (0, pole * blocks), (split, blocks))
        )
    with jax.named_scope("route_first"):
        arrived_first = route(packed_first)

    core = lax.rem(lax.axis_index("node"), 2)
    half = jax.ShapeDtypeStruct((slots // 2, split), BF16)
    same_core, other_core = pl.pallas_call(
        functools.partial(pack_second_kernel, capacity),
        in_specs=[scalar] + [whole] * (1 + len(parts_second)),
        out_shape=[half, half],
        compiler_params=params(),
        cost_estimate=cost(200 * slots * blocks * split, 200 * slots * blocks),
        name="pack_second",
    )(core.reshape(1), place, *parts_second)
    with jax.named_scope("route_second"):
        sibling = lax.ppermute(other_core, "node", [(k, k ^ 1) for k in range(nodes)])
        chips = nodes // 2
        both = jnp.concatenate(
            [x.reshape(chips, capacity, split) for x in (same_core, sibling)], axis=1
        )
        groups = [list(range(c, nodes, 2)) for c in range(2)]
        arrived_second = lax.all_to_all(
            both, "node", 0, 0, axis_index_groups=groups, tiled=True
        ).reshape(slots, split)

    info = pl.pallas_call(
        functools.partial(contract_first_kernel, last, capacity),
        in_specs=[scalar, whole, whole, whole],
        out_shape=jax.ShapeDtypeStruct((8, slots), F32),
        compiler_params=params(),
        cost_estimate=cost(2 * slots * blocks * wide, 2 * slots * blocks),
        name="contract_first",
    )(core.reshape(1), arrived_first, deriv_first, pair_atoms)

    partial_forces = pl.pallas_call(
        force_kernel,
        in_specs=[whole, pl.BlockSpec(memory_space=pltpu.HBM), whole],
        out_shape=jax.ShapeDtypeStruct((3, owners, ATOM_DEV), BF16),
        scratch_shapes=[
            pltpu.VMEM((owners, 3 * ATOM_DEV), F32),
            pltpu.VMEM((3, blocks, split), BF16),
            pltpu.SemaphoreType.DMA((max(1, blocks // 512),)),
        ],
        compiler_params=params(),
        cost_estimate=cost(2 * slots * blocks * split, 2 * slots * blocks),
        name="contract_and_scatter",
    )(arrived_second, pltpu.with_memory_space_constraint(deriv_second, pltpu.HBM), info)

    with jax.named_scope("force_exchange"):
        gathered = lax.all_to_all(
            jnp.transpose(partial_forces, (1, 0, 2)), ("pole", "node"), 0, 0, tiled=True
        )
        return jnp.sum(gathered.astype(F32), axis=0)


def solution(mesh):
    return jax.shard_map(
        body,
        mesh=mesh,
        in_specs=(
            P("pole", "node", None),
            P("node"),
            P("node"),
            P(("pole", "node"), None),
            P(None, ("pole", "node")),
        ),
        out_specs=P(None, ("pole", "node")),
        check_vma=False,
    )
```
